512 devices in a mesh: blk: 16 (over x_lo, y), lane: 32 (over x_hi, z, core).
Axes of the slice: x: 4 (x_hi: 2, x_lo: 2; x = x_hi * 2 + x_lo), y: 8, z: 8, core: 2. Of those that a mesh axis runs over, the one named last changes fastest.
Arguments:
- incident: bfloat16 [16, 4096, 128], P('blk', 'lane'), may hold values from -6 to 6
- geometry: float32 [16, 6, 4096], P('blk', None, 'lane'), may hold values from -30 to 30, as said below
- order: int32 [16, 32, 128], P('blk', 'lane'), may hold values from 0 to 127, each once within a row
- pairs: int32 [16, 32, 2, 192], P('blk', 'lane'), may hold values from 0 to 63, as said below
- counts: int32 [16, 32], P('blk', 'lane'), may hold values from 48 to 192, as said below
Outputs:
- currents: float32 [16, 4096, 128], P('blk', 'lane')
The draws below stay inside these ranges and needn't reach their ends.
Inputs may be any that keep to these rules, and one draw needn't show every extreme that they name: `geometry`: positions and area vectors of facets; area vectors are far smaller than positions. For each device (b, l) the entries i < counts[b, l] are distinct visible pairs, ordered by target block (row 1) non-decreasing; row 0 lies in 0 to 5; entries from counts[b, l] on are in range and carry no interaction. `counts`: some device has all 192 pairs visible.
All inputs are finite; a program needn't handle non-finite values.
Results may differ from the reference program's by a relative error of at most 0.00035.
Values sent between devices are 32-bit elements; how exact they have to be, the bound alone decides.
A program may use at most 64 MiB of HBM per device.

```python
import math
import jax
import jax.numpy as jnp
from jax import lax

BS = 64
FB = 2
SWEEPS = 2
COLS = 128
FPD = 128
CYCLES = 16
LANES = 32
ROWS = 4096
PMAX = 192
N_BLK = 16


def visible_lists(key):
    base = jax.random.fold_in(key, 17)
    key_counts, key_top, key_perm = jax.random.split(base, 3)
    devices_all = CYCLES * LANES
    every = 3 * FB * FB * LANES
    drawn = jax.random.randint(key_counts, (devices_all,), PMAX // 4, PMAX + 1, dtype=jnp.int32)
    busiest = jax.random.randint(key_top, (), 0, devices_all, dtype=jnp.int32)
    drawn = jnp.where(jnp.arange(devices_all, dtype=jnp.int32) == busiest, PMAX, drawn)
    keys = jax.random.split(key_perm, devices_all)
    shuffled = jax.vmap(lambda single: jax.random.permutation(single, every)[:PMAX])(keys).astype(jnp.int32)
    position = jnp.arange(PMAX, dtype=jnp.int32)[None, :]
    marked = jnp.where(position < drawn[:, None], shuffled, shuffled + every)
    ordered = jnp.sort(marked, axis=1) % every
    window = ordered % (3 * FB)
    target = ordered // (3 * FB)
    listed = jnp.stack([window, target], axis=1).reshape(CYCLES, LANES, 2, PMAX)
    return (listed.astype(jnp.int32), drawn.reshape(CYCLES, LANES))


def draw_pairs(key, part):
    return visible_lists(key)[0]


def draw_counts(key, part):
    return visible_lists(key)[1]


def draw_geometry(key, part):
    key_pos, key_area, key_scale = jax.random.split(key, 3)
    factor = jnp.exp(jax.random.uniform(key_scale, (CYCLES, 1, ROWS), jnp.float32, -1.15, 1.15))
    places = 6.0 * jnp.clip(jax.random.normal(key_pos, (CYCLES, 3, ROWS), jnp.float32), -5.0, 5.0)
    areas = 0.03 * jnp.clip(jax.random.normal(key_area, (CYCLES, 3, ROWS), jnp.float32), -4.0, 4.0) * factor
    return jnp.concatenate([places, areas], axis=1)


def block_levels(stream_key, shape, cuts, low, largest):
    level, own = 1.0, jax.random.fold_in(stream_key, 6)
    for dim, shards_of in cuts:
        heights = jnp.exp(jax.random.uniform(jax.random.fold_in(own, dim), (shards_of,), jnp.float32, low / len(cuts), largest / len(cuts)))
        level = level * jnp.repeat(heights, shape[dim] // shards_of).reshape([-1 if axis == dim else 1 for axis in range(len(shape))])
    return level


def centred(key, shape, deviation, most, cuts=(), kind=jnp.bfloat16):
    values = deviation * jax.random.normal(key, shape, jnp.float32)
    if cuts:
        values = values * block_levels(key, shape, cuts, -0.22, 0.18)
    return jnp.clip(values, -most, most).astype(kind)


def setup_inputs(seed: int = 0) -> dict:
    seeds = jax.random.split(jax.random.key(seed), 6)
    return {
        "incident": centred(seeds[0], (CYCLES, ROWS, COLS), 1.0, 6.0, ((0, 16), (1, 32))),
        "geometry": draw_geometry(jax.random.fold_in(seeds[5], 71), 0),
        "order": jax.vmap(lambda own: jax.random.permutation(own, FPD))(jax.random.split(seeds[2], CYCLES * LANES)).reshape((CYCLES, LANES, FPD)).astype(jnp.int32),
        "pairs": draw_pairs(jax.random.fold_in(seeds[5], 71), 0),
        "counts": draw_counts(jax.random.fold_in(seeds[5], 71), 0),
    }


def green_block(target, source):
    width = source.shape[-1]
    tiled = jnp.concatenate([source, source], axis=-1)
    offset = tiled[:, :, None, :] - target[:3, :, :, None]
    radius = jnp.sqrt(lax.optimization_barrier(jnp.sum(offset * offset, axis=0)) + 1.0)
    facing = lax.optimization_barrier(jnp.sum(target[3:, :, :, None] * offset, axis=0)) / (radius * radius)
    phase = jnp.where(jnp.arange(2 * width) >= width, 0.5 * math.pi, 0.0)
    return facing * jnp.cos(2.0 * math.pi * radius + phase)

def apply_block(green, current):
    half = current.shape[-1] // 2
    turned = jnp.concatenate([-current[..., half:], current[..., :half]], axis=-1)
    stacked = jnp.concatenate([current, turned], axis=1)
    return jnp.einsum('gik,gkc->gic', green.astype(jnp.float32), stacked.astype(jnp.float32), precision=lax.Precision.HIGHEST)

def reference(incident, geometry, order, pairs, counts):
    facets = FB * BS
    group = 8
    lane_base = (jnp.arange(LANES, dtype=jnp.int32) * facets)[None, :, None]
    perm = (order + lane_base).reshape(CYCLES, ROWS).astype(jnp.int32)
    blocked_geo = jnp.take_along_axis(geometry, perm[:, None, :], axis=2)
    start = jnp.take_along_axis(incident, perm[:, :, None], axis=1)
    targets_all = blocked_geo.reshape(CYCLES, 6, LANES * FB, BS)

    def field(current):

        def cycle_field(cycle):
            nearby = (cycle + jnp.arange(3, dtype=jnp.int32) - 1) % N_BLK
            near_cur = current[nearby]
            near_geo = blocked_geo[nearby][:, :3]
            cycle_targets = targets_all[cycle]

            def lane_term(lane, total):
                window = lax.dynamic_slice_in_dim(near_cur, (lane * facets).astype(jnp.int32), facets, 1)
                window = window.reshape(3 * FB, BS, COLS)
                source = lax.dynamic_slice_in_dim(near_geo, (lane * facets).astype(jnp.int32), facets, 2)
                source = jnp.transpose(source, (1, 0, 2)).reshape(3, 3 * FB, BS)
                pair_list = pairs[cycle, lane]
                live_count = counts[cycle, lane]

                def group_term(index, acc):
                    first = (index * group).astype(jnp.int32)
                    piece = lax.dynamic_slice_in_dim(pair_list, first, group, 1)
                    live = first + jnp.arange(group, dtype=jnp.int32) < live_count
                    green = green_block(jnp.take(cycle_targets, piece[1], axis=1), jnp.take(source, piece[0], axis=1))
                    contrib = apply_block(green, jnp.take(window, piece[0], axis=0))
                    contrib = jnp.where(live[:, None, None], contrib, 0.0)
                    return acc.at[piece[1]].add(contrib)
                return lax.fori_loop(0, PMAX // group, group_term, total)
            zero = jnp.zeros((LANES * FB, BS, COLS), jnp.float32)
            return lax.fori_loop(0, LANES, lane_term, zero)
        return lax.map(cycle_field, jnp.arange(CYCLES, dtype=jnp.int32)).reshape(CYCLES, ROWS, COLS)
    base = start.astype(jnp.float32)
    current = base
    for sweep in range(SWEEPS - 1):
        current = base + field(current)
    final = base + field(current)
    return jax.vmap(lambda place, values: jnp.zeros_like(values).at[place].set(values))(perm, final)
```

```python
import functools

import jax
import jax.numpy as jnp
from jax import lax
from jax.experimental import pallas as pl
from jax.experimental.pallas import tpu as pltpu
from jax.sharding import PartitionSpec as P

BS = 64
FB = 2
FPD = BS * FB
COLS = 128
INFO = 16
LIST = 256
PMAX = 192
CYC = 3
ROWS = CYC * 2 * FPD

F32 = jnp.float32
BF16 = jnp.bfloat16
MESH = pl.DeviceIdType.MESH
ROUND = 12582912.0
SIN = (4.442867903016683, -7.307443420820961, 3.5947880748152716, -0.7843740225385425)
COS = (
    -1.4142134965649493,
    6.978850988230643,
    -5.7394611705151934,
    1.8835629862356886,
    -0.3106981896782719,
)


def split(value):
    high = value.astype(BF16)
    return high, (value - high.astype(F32)).astype(BF16)


def split3(value):
    high, low = split(value)
    rest = value - high.astype(F32) - low.astype(F32)
    return high, low, rest.astype(BF16)


def dot(a, b):
    return jnp.dot(a, b, preferred_element_type=F32)


def kernel(
    nb,
    nz,
    inc_ref,
    geo_ref,
    order_ref,
    pairs_ref,
    count_ref,
    out_ref,
    geo_in,
    target,
    first,
    second,
    mask,
    weight,
    green_hi,
    green_lo,
    total,
    part_in,
    geo_send,
    geo_recv,
    half_send,
    half_recv,
    ring_send,
    ring_recv,
    part_send,
    part_recv,
):
    blk = lax.axis_index("blk")
    lane = lax.axis_index("lane")
    core = lane % 2
    chip = lane // 2
    z = chip % nz
    x_hi = chip // nz
    reach = nz // 2
    sibling = lane + 1 - 2 * core
    across = (1 - x_hi) * (2 * nz) + z * 2 + core
    right = x_hi * (2 * nz) + ((z + 1) % nz) * 2 + core
    left = x_hi * (2 * nz) + ((z + nz - 1) % nz) * 2 + core

    def cycle(c):
        return (blk + (c - 1) + nb) % nb

    owners = [
        (c, e, (cycle(c), lane if e == 0 else sibling))
        for c, e in ((0, 0), (2, 0), (0, 1), (2, 1), (1, 1))
    ]
    near = [(blk, across), (blk, right), (blk, left)]

    barrier = pltpu.get_barrier_semaphore()
    for device in [d for _, _, d in owners] + near:
        pl.semaphore_signal(barrier, inc=1, device_id=device, device_id_type=MESH)

    facet = lax.broadcasted_iota(jnp.int32, (FPD, FPD), 0)
    placed = jnp.where(order_ref[...] == facet, 1.0, 0.0).astype(F32)
    placed16 = placed.astype(BF16)
    picked16 = jnp.transpose(placed).astype(BF16)
    start = dot(picked16, inc_ref[...])
    first[0, 0:FPD, :] = start
    first[0, FPD : FPD + INFO, :] = jnp.zeros((INFO, COLS), F32)
    geo_in[2] = jnp.full((8, LIST), -1.0, F32)
    pieces = split3(geo_ref[...])
    geo_in[2, 0:6, 0:FPD] = sum(dot(piece, placed16) for piece in pieces)
    live = lax.broadcasted_iota(jnp.int32, (2, PMAX), 1) < count_ref[...]
    geo_in[2, 6:8, 0:PMAX] = jnp.where(live, pairs_ref[...], -1).astype(F32)

    pl.semaphore_wait(barrier, len(owners) + len(near))

    sends = []

    def copy(source, dest, send, recv, device):
        return pltpu.make_async_remote_copy(
            src_ref=source,
            dst_ref=dest,
            send_sem=send,
            recv_sem=recv,
            device_id=device,
            device_id_type=MESH,
        )

    def put(*args):
        made = copy(*args)
        made.start()
        sends.append(made)

    for c, e, device in owners:
        mine = (2 - c) * 2 + e
        put(geo_in.at[2], geo_in.at[mine], geo_send.at[mine], geo_recv.at[mine], device)

    def spread(slot):
        turned = jnp.transpose(geo_in[slot, :, 0:FPD])
        for row in range(6):
            target[row, slot * FPD : (slot + 1) * FPD, :] = jnp.broadcast_to(
                turned[:, row : row + 1], (FPD, FPD)
            )

    total[...] = jnp.zeros(total.shape, F32)
    spread(2)
    for c, e, device in owners:
        slot = c * 2 + e
        copy(
            geo_in.at[2], geo_in.at[slot], geo_send.at[slot], geo_recv.at[slot], device
        ).wait_recv()
        spread(slot)
    for c in range(CYC):
        for row in range(2):
            base = FPD + row * 6 + c * 2
            first[0, base : base + 1, :] = geo_in[c * 2, 6 + row : 7 + row, 0:128]
            first[0, base + 1 : base + 2, :] = geo_in[c * 2, 6 + row : 7 + row, 128:256]
    first[0, FPD + 12 : FPD + 15, :] = geo_in[2, 0:3, 0:FPD]

    def ring_sem(sweep, way, h, d):
        return ((sweep * 2 + way) * 2 + h) * reach + d

    def ring_copy(sweep, buf, way, h, d):
        if way == 0:
            here, there, device = (nz - d) % nz, nz - d - 1, (blk, right)
        else:
            here, there, device = d, d + 1, (blk, left)
        height = buf.shape[1]
        rows = pl.ds(0, height)
        if d == reach - 1:
            rows = pl.ds(way * (height // 2), height // 2)
        sem = ring_sem(sweep, way, h, d)
        return (
            buf.at[h * nz + here, rows],
            buf.at[h * nz + there, rows],
            ring_send.at[sem],
            ring_recv.at[sem],
            device,
        )

    def gather(sweep, buf, work):
        def forward(h, d):
            for way in range(2):
                put(*ring_copy(sweep, buf, way, h, d))

        def arrive(h, d):
            for way in range(2):
                copy(*ring_copy(sweep, buf, way, h, d)).wait_recv()

        cross = (buf.at[0], buf.at[nz], half_send.at[sweep], half_recv.at[sweep], (blk, across))
        put(*cross)
        forward(0, 0)
        work(0, 1, 1)
        copy(*cross).wait_recv()
        forward(1, 0)
        work(nz, 1, 1)
        for d in range(1, reach):
            for h in range(2):
                arrive(h, d - 1)
                forward(h, d)
                work(h * nz + d, nz - 2 * d, 2)
        for h in range(2):
            arrive(h, reach - 1)
        work(reach, nz, 2)

    lane_half = lax.broadcasted_iota(jnp.int32, (INFO, COLS), 1) // BS
    wanted_row = lax.broadcasted_iota(jnp.int32, (INFO, COLS), 0)
    wanted_part = wanted_row % 4
    wanted = (2 * (2 * chip + (core + wanted_part // 2) % 2) + wanted_part % 2).astype(F32)
    wanted = [jnp.where(wanted_row // 4 == c, wanted, -5.0) for c in range(CYC)]
    sign = jnp.where(lax.broadcasted_iota(jnp.int32, (FPD, COLS), 1) < BS, -1.0, 1.0)

    def stacked(current):
        swapped = jnp.concatenate([current[:, BS:], current[:, :BS]], axis=1)
        return current, swapped * sign

    def visible(slot):
        seen = [jnp.zeros((INFO, COLS), F32), jnp.zeros((INFO, COLS), F32)]
        info = first[slot, FPD : FPD + INFO, :]
        for row in range(2 * CYC):
            c = row // 2
            hit = info[6 + row : 7 + row, :] == wanted[c]
            for side in range(2):
                same = info[row : row + 1, :] == float(2 * (2 - c) + side)
                seen[side] += jnp.where(hit & same, 1.0, 0.0)
        sums = [jnp.sum(s, axis=1, keepdims=True) for s in seen]
        mask[...] = jnp.where(lane_half == 0, sums[0], sums[1])

    def green_work(base, stride, count):
        def one(j, _):
            slot = base + j * stride
            upper, lower = stacked(first[slot, 0:FPD, :])
            weight[0:FPD, 0:COLS] = upper.astype(BF16)
            weight[FPD : 2 * FPD, 0:COLS] = lower.astype(BF16)
            visible(slot)

            def chunk(i, _):
                rows = pl.ds(pl.multiple_of(i * FPD, FPD), FPD)
                place = first[slot, FPD + 12 : FPD + 15, :]
                offset = [place[k : k + 1, :] - target[k, rows, :] for k in range(3)]
                square = offset[0] * offset[0] + offset[1] * offset[1]
                square = square + offset[2] * offset[2] + 1.0
                inverse = lax.rsqrt(square)
                radius = square * inverse
                facing = sum(target[3 + k, rows, :] * offset[k] for k in range(3))
                shown = mask[pl.ds(2 * i, 2), :]
                shown = jnp.concatenate(
                    [jnp.broadcast_to(shown[k : k + 1, :], (BS, COLS)) for k in range(FB)], axis=0
                )
                facing = facing * shown * (inverse * inverse)
                turn = radius - ((radius + ROUND) - ROUND)
                power = turn * turn
                sine = turn * (((SIN[3] * power + SIN[2]) * power + SIN[1]) * power + SIN[0])
                cosine = COS[4] * power + COS[3]
                cosine = ((cosine * power + COS[2]) * power + COS[1]) * power + COS[0]
                real_hi, real_lo = split(facing * (1.0 - sine * sine))
                imag_hi, imag_lo = split(facing * (sine * cosine))
                high = jnp.concatenate([real_hi, imag_hi], axis=1)
                low = jnp.concatenate([real_lo, imag_lo], axis=1)
                green_hi[slot, rows, :] = high
                green_lo[slot, rows, :] = low
                term = dot(jnp.concatenate([high, low], axis=0), weight[:, 0:COLS])
                total[0, rows, :] += term[0:FPD] + term[FPD : 2 * FPD]
                return 0

            lax.fori_loop(0, 2 * CYC, chunk, 0)
            return 0

        lax.fori_loop(0, count, one, 0)

    def field_work(base, stride, count):
        def one(j, _):
            slot = base + j * stride
            for half, value in enumerate(stacked(second[slot])):
                high, low = split(value)
                weight[half * FPD : (half + 1) * FPD, 0:COLS] = high
                weight[half * FPD : (half + 1) * FPD, COLS : 2 * COLS] = low

            def chunk(i, _):
                rows = pl.ds(pl.multiple_of(i * 2 * FPD, 2 * FPD), 2 * FPD)
                term = dot(green_hi[slot, rows, :], weight[...])
                rest = dot(green_lo[slot, rows, :], weight[:, 0:COLS])
                total[1, rows, :] += term[:, 0:COLS] + (term[:, COLS:] + rest)
                return 0

            lax.fori_loop(0, CYC, chunk, 0)
            return 0

        lax.fori_loop(0, count, one, 0)

    def exchange(sweep):
        def args(c, e, device):
            index = (0, 1, None, 2, 3, 4)[(2 - c) * 2 + e]
            return (
                total.at[sweep, pl.ds((c * 2 + e) * FPD, FPD)],
                part_in.at[sweep, index],
                part_send.at[sweep * 5 + index],
                part_recv.at[sweep * 5 + index],
                device,
            )

        for c, e, device in owners:
            put(*args(c, e, device))
        result = start + total[sweep, 2 * FPD : 3 * FPD, :]
        for c, e, device in owners:
            copy(*args(c, e, device)).wait_recv()
        for index in range(5):
            result = result + part_in[sweep, index]
        return result

    gather(0, first, green_work)
    second[0] = exchange(0)
    gather(1, second, field_work)
    final = exchange(1)
    out_ref[...] = sum(dot(placed16, piece) for piece in split3(final))

    for made in sends:
        made.wait_send()


def per_device(incident, geometry, order, pairs, counts):
    nb = lax.axis_size("blk")
    nz = lax.axis_size("lane") // 4
    reach = nz // 2
    vmem = pl.BlockSpec(memory_space=pltpu.VMEM)
    out = pl.pallas_call(
        functools.partial(kernel, nb, nz),
        out_shape=jax.ShapeDtypeStruct((FPD, COLS), F32),
        in_specs=[vmem] * 5,
        out_specs=vmem,
        scratch_shapes=[
            pltpu.VMEM((2 * CYC, 8, LIST), F32),
            pltpu.VMEM((6, ROWS, FPD), F32),
            pltpu.VMEM((2 * nz, FPD + INFO, COLS), F32),
            pltpu.VMEM((2 * nz, FPD, COLS), F32),
            pltpu.VMEM((INFO, COLS), F32),
            pltpu.VMEM((2 * FPD, 2 * COLS), BF16),
            pltpu.VMEM((2 * nz, ROWS, 2 * FPD), BF16),
            pltpu.VMEM((2 * nz, ROWS, 2 * FPD), BF16),
            pltpu.VMEM((2, ROWS, COLS), F32),
            pltpu.VMEM((2, 5, FPD, COLS), F32),
            pltpu.SemaphoreType.DMA((6,)),
            pltpu.SemaphoreType.DMA((6,)),
            pltpu.SemaphoreType.DMA((2,)),
            pltpu.SemaphoreType.DMA((2,)),
            pltpu.SemaphoreType.DMA((8 * reach,)),
            pltpu.SemaphoreType.DMA((8 * reach,)),
            pltpu.SemaphoreType.DMA((10,)),
            pltpu.SemaphoreType.DMA((10,)),
        ],
        compiler_params=pltpu.CompilerParams(
            collective_id=0, has_side_effects=True, vmem_limit_bytes=40 * 2**20
        ),
        name="sweeps",
    )(incident[0], geometry[0], order[0], pairs[0, 0], counts)
    return out[None]


def solution(mesh):
    placed = (
        P("blk", "lane", None),
        P("blk", None, "lane"),
        P("blk", "lane", None),
        P("blk", "lane", None, None),
        P("blk", "lane"),
    )
    return jax.shard_map(
        per_device, mesh=mesh, in_specs=placed, out_specs=P("blk", "lane", None), check_vma=False
    )
```

```python
import functools

import jax
import jax.numpy as jnp
from jax import lax
from jax.experimental import pallas as pl
from jax.experimental.pallas import tpu as pltpu
from jax.sharding import PartitionSpec as P

BS = 64
FB = 2
FPD = BS * FB
COLS = 128
INFO = 16
LIST = 256
PMAX = 192
CYC = 3
ROWS = CYC * 2 * FPD

F32 = jnp.float32
BF16 = jnp.bfloat16
MESH = pl.DeviceIdType.MESH
ROUND = 12582912.0
SIN = (4.442867903016683, -7.307443420820961, 3.5947880748152716, -0.7843740225385425)
COS = (
    -1.4142134965649493,
    6.978850988230643,
    -5.7394611705151934,
    1.8835629862356886,
    -0.3106981896782719,
)


def split(value):
    high = value.astype(BF16)
    return high, (value - high.astype(F32)).astype(BF16)


def split3(value):
    high, low = split(value)
    rest = value - high.astype(F32) - low.astype(F32)
    return high, low, rest.astype(BF16)


def dot(a, b):
    return jnp.dot(a, b, preferred_element_type=F32)


def kernel(
    nb,
    nz,
    inc_ref,
    geo_ref,
    order_ref,
    pairs_ref,
    count_ref,
    out_ref,
    geo_in,
    target,
    current,
    info,
    mask,
    weight,
    green_hi,
    green_lo,
    total,
    part_in,
    geo_send,
    geo_recv,
    info_send,
    info_recv,
    ring_send,
    ring_recv,
    part_send,
    part_recv,
):
    blk = lax.axis_index("blk")
    lane = lax.axis_index("lane")
    core = lane % 2
    chip = lane // 2
    z = chip % nz
    x_hi = chip // nz
    sibling = lane + 1 - 2 * core
    across = (blk, (1 - x_hi) * (2 * nz) + z * 2 + core)

    def along(step):
        return (blk, x_hi * (2 * nz) + ((z + step + nz) % nz) * 2 + core)

    def cycle(c):
        return (blk + (c - 1) + nb) % nb

    owners = [
        (c, e, (cycle(c), lane if e == 0 else sibling))
        for c, e in ((0, 0), (2, 0), (0, 1), (2, 1), (1, 1))
    ]
    near = [across, along(1), along(-1), along(2), along(-2)]

    barrier = pltpu.get_barrier_semaphore()
    for device in [d for _, _, d in owners] + near:
        pl.semaphore_signal(barrier, inc=1, device_id=device, device_id_type=MESH)

    facet = lax.broadcasted_iota(jnp.int32, (FPD, FPD), 0)
    placed = jnp.where(order_ref[...] == facet, 1.0, 0.0).astype(F32)
    placed16 = placed.astype(BF16)
    picked16 = jnp.transpose(placed).astype(BF16)
    start = dot(picked16, inc_ref[...])
    current[0, 0] = start
    info[0] = jnp.zeros((INFO, COLS), F32)
    geo_in[2] = jnp.full((8, LIST), -1.0, F32)
    pieces = split3(geo_ref[...])
    geo_in[2, 0:6, 0:FPD] = sum(dot(piece, placed16) for piece in pieces)
    live = lax.broadcasted_iota(jnp.int32, (2, PMAX), 1) < count_ref[...]
    geo_in[2, 6:8, 0:PMAX] = jnp.where(live, pairs_ref[...], -1).astype(F32)

    pl.semaphore_wait(barrier, len(owners) + len(near))

    sends = []

    def copy(source, dest, send, recv, device):
        return pltpu.make_async_remote_copy(
            src_ref=source,
            dst_ref=dest,
            send_sem=send,
            recv_sem=recv,
            device_id=device,
            device_id_type=MESH,
        )

    def put(place, *which):
        copy(*place(*which)).start()
        sends.append((place, which))

    def slot_of(h, d):
        return h * nz + d % nz

    full, top, bottom = (pl.ds(0, FPD), pl.ds(0, FPD // 2), pl.ds(FPD // 2, FPD // 2))
    hops = [
        ((0, 0), (0, -2), full, along(2)),
        ((0, 0), (0, 2), full, along(-2)),
        ((0, 0), (0, -1), full, along(1)),
        ((0, 0), (0, 1), full, along(-1)),
        ((0, 0), (1, 0), full, across),
        ((0, -2), (0, -3), full, along(1)),
        ((0, 2), (0, 3), full, along(-1)),
        ((0, -2), (0, 4), top, along(2)),
        ((0, 2), (0, 4), bottom, along(-2)),
        ((0, -2), (1, -2), full, across),
        ((0, 2), (1, 2), full, across),
        ((0, -1), (1, -1), full, across),
        ((0, 1), (1, 1), full, across),
        ((1, -2), (1, -3), full, along(1)),
        ((1, 2), (1, 3), full, along(-1)),
        ((0, 4), (1, 4), full, across),
    ]

    def hop(sweep, k):
        source, dest, rows, device = hops[k]
        return (
            current.at[sweep, slot_of(*source), rows],
            current.at[sweep, slot_of(*dest), rows],
            ring_send.at[sweep * len(hops) + k],
            ring_recv.at[sweep * len(hops) + k],
            device,
        )

    def pass_on(sweep, *which):
        for k in which:
            put(hop, sweep, k)

    def arrive(sweep, *which):
        for k in which:
            copy(*hop(sweep, k)).wait_recv()

    def note(source, dest, device):
        there = slot_of(*dest)
        return (
            info.at[slot_of(*source)],
            info.at[there],
            info_send.at[there],
            info_recv.at[there],
            device,
        )

    def tell(*steps):
        for step in steps:
            put(note, (0, 0), (0, -step), along(step))

    def told(h, *distances):
        for d in distances:
            if h == 0:
                copy(*note((0, 0), (0, d), along(-d))).wait_recv()
                put(note, (0, d), (1, d), across)
            else:
                copy(*note((0, d), (1, d), across)).wait_recv()

    def place_of(slot, device):
        return geo_in.at[2], geo_in.at[slot], geo_send.at[slot], geo_recv.at[slot], device

    for c, e, device in owners:
        put(place_of, (2 - c) * 2 + e, device)
    pass_on(0, 0, 1, 2, 3, 4)

    def spread(slot):
        turned = jnp.transpose(geo_in[slot, :, 0:FPD])
        for row in range(6):
            target[row, slot * FPD : (slot + 1) * FPD, :] = jnp.broadcast_to(
                turned[:, row : row + 1], (FPD, FPD)
            )

    total[...] = jnp.zeros(total.shape, F32)
    spread(2)
    for c, e, device in owners:
        copy(*place_of(c * 2 + e, device)).wait_recv()
    for c in range(CYC):
        for row in range(2):
            base = row * 6 + c * 2
            info[0, base : base + 1, :] = geo_in[c * 2, 6 + row : 7 + row, 0:128]
            info[0, base + 1 : base + 2, :] = geo_in[c * 2, 6 + row : 7 + row, 128:256]
    info[0, 12:15, :] = geo_in[2, 0:3, 0:FPD]
    tell(1, -1, 2, -2)
    put(note, (0, 0), (1, 0), across)

    lane_half = lax.broadcasted_iota(jnp.int32, (INFO, COLS), 1) // BS
    wanted_row = lax.broadcasted_iota(jnp.int32, (INFO, COLS), 0)
    wanted_part = wanted_row % 4
    wanted = (2 * (2 * chip + (core + wanted_part // 2) % 2) + wanted_part % 2).astype(F32)
    wanted = [jnp.where(wanted_row // 4 == c, wanted, -5.0) for c in range(CYC)]
    sign = jnp.where(lax.broadcasted_iota(jnp.int32, (FPD, COLS), 1) < BS, -1.0, 1.0)

    def stacked(value):
        swapped = jnp.concatenate([value[:, BS:], value[:, :BS]], axis=1)
        return value, swapped * sign

    def visible(slot):
        seen = [jnp.zeros((INFO, COLS), F32), jnp.zeros((INFO, COLS), F32)]
        told_rows = info[slot]
        for row in range(2 * CYC):
            c = row // 2
            hit = told_rows[6 + row : 7 + row, :] == wanted[c]
            for side in range(2):
                same = told_rows[row : row + 1, :] == float(2 * (2 - c) + side)
                seen[side] += jnp.where(hit & same, 1.0, 0.0)
        sums = [jnp.sum(s, axis=1, keepdims=True) for s in seen]
        mask[...] = jnp.where(lane_half == 0, sums[0], sums[1])

    def make_green(slot, i):
        place = info[slot, 12:15, :]
        for part in range(2 * FB):
            rows = pl.ds(pl.multiple_of((i * 2 * FB + part) * BS, BS), BS)
            offset = [place[k : k + 1, :] - target[k, rows, :] for k in range(3)]
            square = offset[0] * offset[0] + offset[1] * offset[1]
            square = square + offset[2] * offset[2] + 1.0
            inverse = lax.rsqrt(square)
            radius = square * inverse
            facing = sum(target[3 + k, rows, :] * offset[k] for k in range(3))
            facing = facing * mask[pl.ds(2 * FB * i + part, 1), :] * (inverse * inverse)
            turn = radius - ((radius + ROUND) - ROUND)
            power = turn * turn
            sine = turn * (((SIN[3] * power + SIN[2]) * power + SIN[1]) * power + SIN[0])
            cosine = COS[4] * power + COS[3]
            cosine = ((cosine * power + COS[2]) * power + COS[1]) * power + COS[0]
            pieces = split(facing * (1.0 - sine * sine)), split(facing * (sine * cosine))
            for half in range(2):
                lanes = pl.ds(half * FPD, FPD)
                green_hi[slot, rows, lanes], green_lo[slot, rows, lanes] = pieces[half]

    def weigh_start(slot):
        for half, value in enumerate(stacked(current[0, slot])):
            weight[half * FPD : (half + 1) * FPD, 0:COLS] = value.astype(BF16)

    def add_start(slot, i):
        rows = pl.ds(pl.multiple_of(i * 2 * FPD, 2 * FPD), 2 * FPD)
        both = jnp.concatenate([green_hi[slot, rows, :], green_lo[slot, rows, :]], axis=0)
        term = dot(both, weight[:, 0:COLS])
        total[0, rows, :] += term[0 : 2 * FPD] + term[2 * FPD :]

    def add_swept(slot):
        for half, value in enumerate(stacked(current[1, slot])):
            high, low = split(value)
            weight[half * FPD : (half + 1) * FPD, 0:COLS] = high
            weight[half * FPD : (half + 1) * FPD, COLS : 2 * COLS] = low
        term = dot(green_hi[slot], weight[...])
        rest = dot(green_lo[slot], weight[:, 0:COLS])
        total[1] += term[:, 0:COLS] + (term[:, COLS:] + rest)

    def picked(order, n):
        return sum(jnp.int32(n == k) * slot_of(*place) for k, place in enumerate(order))

    def chunks(body):
        def one(i, _):
            body(i)
            return 0

        lax.fori_loop(0, CYC, one, 0)

    def partial_of(sweep, c, e, device):
        index = (0, 1, None, 2, 3, 4)[(2 - c) * 2 + e]
        return (
            total.at[sweep, pl.ds((c * 2 + e) * FPD, FPD)],
            part_in.at[sweep, index],
            part_send.at[sweep * 5 + index],
            part_recv.at[sweep * 5 + index],
            device,
        )

    def exchange(sweep):
        for owner in owners:
            put(partial_of, sweep, *owner)
        result = start + total[sweep, 2 * FPD : 3 * FPD, :]
        for owner in owners:
            copy(*partial_of(sweep, *owner)).wait_recv()
        for index in range(5):
            result = result + part_in[sweep, index]
        return result

    arrive(0, 0, 1)
    pass_on(0, 5, 6, 7, 8, 9, 10)
    arrive(0, 2, 3)
    pass_on(0, 11, 12)
    tell(3, -3, 4)
    for slot in (0, 1, 3, 4, 5):
        spread(slot)

    order = [(0, 0), (0, -1), (0, 1), (0, -2), (0, 2), (0, -3), (0, 3), (0, 4)]
    order += [(1, 0), (1, -1), (1, 1), (1, -2), (1, 2), (1, -3), (1, 3), (1, 4)]

    def start_step(n, _):
        @pl.when(n == 1)
        def _():
            told(0, -1, 1)

        @pl.when(n == 3)
        def _():
            told(0, -2, 2)
            arrive(0, 9, 10)
            pass_on(0, 13, 14)

        @pl.when(n == 4)
        def _():
            arrive(0, 7, 8)
            pass_on(0, 15)

        @pl.when(n == 5)
        def _():
            told(0, -3, 3, 4)
            arrive(0, 5, 6)

        @pl.when(n == 8)
        def _():
            told(1, 0)
            arrive(0, 4)

        @pl.when(n == 9)
        def _():
            told(1, -1, 1)
            arrive(0, 11, 12)

        @pl.when(n == 11)
        def _():
            told(1, -2, 2)

        @pl.when(n == 13)
        def _():
            told(1, -3, 3)
            arrive(0, 13, 14)

        @pl.when(n == 15)
        def _():
            told(1, 4)

        slot = picked(order, n)
        prior = picked(order, n - 1)
        weigh_start(prior)
        visible(slot)

        def both(i):
            add_start(prior, i)
            make_green(slot, i)

        chunks(both)
        return 0

    visible(0)
    chunks(functools.partial(make_green, 0))
    lax.fori_loop(1, 2 * nz, start_step, 0)
    arrive(0, 15)
    weigh_start(slot_of(1, 4))
    chunks(functools.partial(add_start, slot_of(1, 4)))

    swept = [(0, 0), (0, -1), (0, 1), (0, -2), (0, 2), (1, 0), (1, -1), (1, 1)]
    swept += [(0, -3), (0, 3), (1, -2), (1, 2), (0, 4), (1, -3), (1, 3), (1, 4)]

    def swept_step(n, _):
        @pl.when(n == 1)
        def _():
            arrive(1, 2, 3)
            pass_on(1, 11, 12)
            arrive(1, 0, 1)
            pass_on(1, 5, 6, 7, 8, 9, 10)

        @pl.when(n == 5)
        def _():
            arrive(1, 4)

        @pl.when(n == 6)
        def _():
            arrive(1, 9, 10)
            pass_on(1, 13, 14)
            arrive(1, 7, 8)
            pass_on(1, 15)
            arrive(1, 11, 12)

        @pl.when(n == 8)
        def _():
            arrive(1, 5, 6)

        @pl.when(n == 13)
        def _():
            arrive(1, 13, 14)

        @pl.when(n == 15)
        def _():
            arrive(1, 15)

        add_swept(picked(swept, n))
        return 0

    current[1, 0] = exchange(0)
    pass_on(1, 0, 1, 2, 3, 4)
    lax.fori_loop(0, 2 * nz, swept_step, 0)
    final = exchange(1)
    out_ref[...] = sum(dot(placed16, piece) for piece in split3(final))

    for place, which in sends:
        copy(*place(*which)).wait_send()


def per_device(incident, geometry, order, pairs, counts):
    nb = lax.axis_size("blk")
    nz = lax.axis_size("lane") // 4
    vmem = pl.BlockSpec(memory_space=pltpu.VMEM)
    out = pl.pallas_call(
        functools.partial(kernel, nb, nz),
        out_shape=jax.ShapeDtypeStruct((FPD, COLS), F32),
        in_specs=[vmem] * 5,
        out_specs=vmem,
        scratch_shapes=[
            pltpu.VMEM((2 * CYC, 8, LIST), F32),
            pltpu.VMEM((6, ROWS, FPD), F32),
            pltpu.VMEM((2, 2 * nz, FPD, COLS), F32),
            pltpu.VMEM((2 * nz, INFO, COLS), F32),
            pltpu.VMEM((INFO, COLS), F32),
            pltpu.VMEM((2 * FPD, 2 * COLS), BF16),
            pltpu.VMEM((2 * nz, ROWS, 2 * FPD), BF16),
            pltpu.VMEM((2 * nz, ROWS, 2 * FPD), BF16),
            pltpu.VMEM((2, ROWS, COLS), F32),
            pltpu.VMEM((2, 5, FPD, COLS), F32),
            pltpu.SemaphoreType.DMA((6,)),
            pltpu.SemaphoreType.DMA((6,)),
            pltpu.SemaphoreType.DMA((2 * nz,)),
            pltpu.SemaphoreType.DMA((2 * nz,)),
            pltpu.SemaphoreType.DMA((32,)),
            pltpu.SemaphoreType.DMA((32,)),
            pltpu.SemaphoreType.DMA((10,)),
            pltpu.SemaphoreType.DMA((10,)),
        ],
        compiler_params=pltpu.CompilerParams(
            collective_id=0, has_side_effects=True, vmem_limit_bytes=40 * 2**20
        ),
        name="sweeps",
    )(incident[0], geometry[0], order[0], pairs[0, 0], counts)
    return out[None]


def solution(mesh):
    placed = (
        P("blk", "lane", None),
        P("blk", None, "lane"),
        P("blk", "lane", None),
        P("blk", "lane", None, None),
        P("blk", "lane"),
    )
    return jax.shard_map(
        per_device, mesh=mesh, in_specs=placed, out_specs=P("blk", "lane", None), check_vma=False
    )
```

```python
import functools

import jax
import jax.numpy as jnp
from jax import lax
from jax.experimental import pallas as pl
from jax.experimental.pallas import tpu as pltpu
from jax.sharding import PartitionSpec as P

BS = 64
FB = 2
FPD = BS * FB
COLS = 128
INFO = 16
LIST = 256
PMAX = 192
CYC = 3
ROWS = CYC * 2 * FPD

F32 = jnp.float32
BF16 = jnp.bfloat16
MESH = pl.DeviceIdType.MESH
ROUND = 12582912.0
SIN = (4.442867903016683, -7.307443420820961, 3.5947880748152716, -0.7843740225385425)
COS = (
    -1.4142134965649493,
    6.978850988230643,
    -5.7394611705151934,
    1.8835629862356886,
    -0.3106981896782719,
)


def split(value):
    high = value.astype(BF16)
    return high, (value - high.astype(F32)).astype(BF16)


def split3(value):
    high, low = split(value)
    rest = value - high.astype(F32) - low.astype(F32)
    return high, low, rest.astype(BF16)


def dot(a, b):
    return jnp.dot(a, b, preferred_element_type=F32)


def kernel(
    nb,
    nz,
    inc_ref,
    geo_ref,
    order_ref,
    pairs_ref,
    count_ref,
    out_ref,
    geo_in,
    target,
    current,
    info,
    mask,
    weight,
    green_hi,
    green_lo,
    total,
    part_in,
    geo_send,
    geo_recv,
    info_send,
    info_recv,
    ring_send,
    ring_recv,
    part_send,
    part_recv,
):
    blk = lax.axis_index("blk")
    lane = lax.axis_index("lane")
    core = lane % 2
    chip = lane // 2
    z = chip % nz
    x_hi = chip // nz
    sibling = lane + 1 - 2 * core
    across = (blk, (1 - x_hi) * (2 * nz) + z * 2 + core)

    steps = {
        step: (blk, x_hi * (2 * nz) + ((z + step + nz) % nz) * 2 + core)
        for step in (1, -1, 2, -2, 3, -3, 4)
    }

    def along(step):
        return steps[step]

    def cycle(c):
        return (blk + (c - 1) + nb) % nb

    owners = [
        (c, e, (cycle(c), lane if e == 0 else sibling))
        for c, e in ((0, 0), (2, 0), (0, 1), (2, 1), (1, 1))
    ]
    near = [across, along(1), along(-1), along(2), along(-2)]

    barrier = pltpu.get_barrier_semaphore()
    for device in [d for _, _, d in owners] + near:
        pl.semaphore_signal(barrier, inc=1, device_id=device, device_id_type=MESH)

    facet = lax.broadcasted_iota(jnp.int32, (FPD, FPD), 0)
    placed = jnp.where(order_ref[...] == facet, 1.0, 0.0).astype(F32)
    placed16 = placed.astype(BF16)
    picked16 = jnp.transpose(placed).astype(BF16)
    start = dot(picked16, inc_ref[...])
    current[0, 0] = start
    info[0] = jnp.zeros((INFO, COLS), F32)
    geo_in[2] = jnp.full((8, LIST), -1.0, F32)
    pieces = split3(geo_ref[...])
    geo_in[2, 0:6, 0:FPD] = sum(dot(piece, placed16) for piece in pieces)
    live = lax.broadcasted_iota(jnp.int32, (2, PMAX), 1) < count_ref[...]
    geo_in[2, 6:8, 0:PMAX] = jnp.where(live, pairs_ref[...], -1).astype(F32)

    pl.semaphore_wait(barrier, len(owners) + len(near))

    sends = []

    def copy(source, dest, send, recv, device):
        return pltpu.make_async_remote_copy(
            src_ref=source,
            dst_ref=dest,
            send_sem=send,
            recv_sem=recv,
            device_id=device,
            device_id_type=MESH,
        )

    def put(place, *which):
        copy(*place(*which)).start()
        sends.append((place, which))

    slots = [(0, 0), (0, -1), (0, 1), (0, -2), (0, 2), (1, 0), (1, -1), (1, 1)]
    slots += [(1, -2), (1, 2), (0, -3), (0, 3), (0, 4), (1, -3), (1, 3), (1, 4)]

    def slot_of(h, d):
        return slots.index((h, 4 if d == -4 else d))

    full, top, bottom = (0, FPD), (0, FPD // 2), (FPD // 2, FPD // 2)
    hops = [
        ((0, 0), (0, -2), full, along(2)),
        ((0, 0), (0, 2), full, along(-2)),
        ((0, 0), (0, -1), full, along(1)),
        ((0, 0), (0, 1), full, along(-1)),
        ((0, 0), (1, 0), full, across),
        ((0, -2), (0, -3), full, along(1)),
        ((0, 2), (0, 3), full, along(-1)),
        ((0, -2), (0, 4), top, along(2)),
        ((0, 2), (0, 4), bottom, along(-2)),
        ((0, -2), (1, -2), full, across),
        ((0, 2), (1, 2), full, across),
        ((0, -1), (1, -1), full, across),
        ((0, 1), (1, 1), full, across),
        ((1, -2), (1, -3), full, along(1)),
        ((1, 2), (1, 3), full, along(-1)),
        ((0, 4), (1, 4), full, across),
    ]

    halves = []
    for source, dest, (base, height), device in hops:
        for part in range(2):
            rows = (base + part * height // 2, height // 2)
            halves.append((source, dest, rows, device))

    def half(part, *which):
        return [2 * k + part for k in which]

    def hop(sweep, k):
        source, dest, rows, device = (hops, halves)[sweep][k]
        sem = sweep * len(hops) + k
        return (
            current.at[sweep, slot_of(*source), pl.ds(*rows)],
            current.at[sweep, slot_of(*dest), pl.ds(*rows)],
            ring_send.at[sem],
            ring_recv.at[sem],
            device,
        )

    def pass_on(sweep, *which):
        for k in which:
            put(hop, sweep, k)

    def arrive(sweep, *which):
        for k in which:
            copy(*hop(sweep, k)).wait_recv()

    def note(source, dest, device):
        there = slot_of(*dest)
        return (
            info.at[slot_of(*source)],
            info.at[there],
            info_send.at[there],
            info_recv.at[there],
            device,
        )

    def tell(*steps):
        for step in steps:
            put(note, (0, 0), (0, -step), along(step))

    def told(h, *distances):
        for d in distances:
            if h == 0:
                copy(*note((0, 0), (0, d), across)).wait_recv()
                put(note, (0, d), (1, d), across)
            else:
                copy(*note((0, d), (1, d), across)).wait_recv()

    def place_of(slot, device):
        return geo_in.at[2], geo_in.at[slot], geo_send.at[slot], geo_recv.at[slot], device

    for c, e, device in owners:
        put(place_of, (2 - c) * 2 + e, device)
    pass_on(0, 0, 1, 2, 3, 4)

    def spread(slot):
        turned = jnp.transpose(geo_in[slot, :, 0:FPD])
        for row in range(6):
            target[row, slot * FPD : (slot + 1) * FPD, :] = jnp.broadcast_to(
                turned[:, row : row + 1], (FPD, FPD)
            )

    total[...] = jnp.zeros(total.shape, F32)
    spread(2)
    for c, e, device in owners:
        copy(*place_of(c * 2 + e, device)).wait_recv()
    for c in range(CYC):
        for row in range(2):
            base = row * 6 + c * 2
            info[0, base : base + 1, :] = geo_in[c * 2, 6 + row : 7 + row, 0:128]
            info[0, base + 1 : base + 2, :] = geo_in[c * 2, 6 + row : 7 + row, 128:256]
    info[0, 12:15, :] = geo_in[2, 0:3, 0:FPD]
    tell(1, -1, 2, -2)
    put(note, (0, 0), (1, 0), across)

    lane_half = lax.broadcasted_iota(jnp.int32, (INFO, COLS), 1) // BS
    wanted_row = lax.broadcasted_iota(jnp.int32, (INFO, COLS), 0)
    wanted_part = wanted_row % 4
    wanted = (2 * (2 * chip + (core + wanted_part // 2) % 2) + wanted_part % 2).astype(F32)
    wanted = [jnp.where(wanted_row // 4 == c, wanted, -5.0) for c in range(CYC)]
    sign = jnp.where(lax.broadcasted_iota(jnp.int32, (FPD, COLS), 1) < BS, -1.0, 1.0)

    def stacked(value):
        swapped = jnp.concatenate([value[:, BS:], value[:, :BS]], axis=1)
        return value, swapped * sign

    def visible(slot):
        seen = [jnp.zeros((INFO, COLS), F32), jnp.zeros((INFO, COLS), F32)]
        told_rows = info[slot]
        for row in range(2 * CYC):
            c = row // 2
            hit = told_rows[6 + row : 7 + row, :] == wanted[c]
            for side in range(2):
                same = told_rows[row : row + 1, :] == float(2 * (2 - c) + side)
                seen[side] += jnp.where(hit & same, 1.0, 0.0)
        sums = [jnp.sum(s, axis=1, keepdims=True) for s in seen]
        mask[...] = jnp.where(lane_half == 0, sums[0], sums[1])

    def make_green(slot, i):
        place = info[slot, 12:15, :]
        for part in range(2 * FB):
            rows = pl.ds(pl.multiple_of((i * 2 * FB + part) * BS, BS), BS)
            offset = [place[k : k + 1, :] - target[k, rows, :] for k in range(3)]
            square = offset[0] * offset[0] + offset[1] * offset[1]
            square = square + offset[2] * offset[2] + 1.0
            inverse = lax.rsqrt(square)
            radius = square * inverse
            facing = sum(target[3 + k, rows, :] * offset[k] for k in range(3))
            facing = facing * mask[pl.ds(2 * FB * i + part, 1), :] * (inverse * inverse)
            turn = radius - ((radius + ROUND) - ROUND)
            power = turn * turn
            sine = turn * (((SIN[3] * power + SIN[2]) * power + SIN[1]) * power + SIN[0])
            cosine = COS[4] * power + COS[3]
            cosine = ((cosine * power + COS[2]) * power + COS[1]) * power + COS[0]
            pieces = split(facing * (1.0 - sine * sine)), split(facing * (sine * cosine))
            for half in range(2):
                lanes = pl.ds(half * FPD, FPD)
                green_hi[slot, rows, lanes], green_lo[slot, rows, lanes] = pieces[half]

    def weigh_start(slot):
        for half, value in enumerate(stacked(current[0, slot])):
            weight[half * FPD : (half + 1) * FPD, 0:COLS] = value.astype(BF16)

    def add_start(slot, i):
        rows = pl.ds(pl.multiple_of(i * 2 * FPD, 2 * FPD), 2 * FPD)
        both = jnp.concatenate([green_hi[slot, rows, :], green_lo[slot, rows, :]], axis=0)
        term = dot(both, weight[:, 0:COLS])
        total[0, rows, :] += term[0 : 2 * FPD] + term[2 * FPD :]

    def add_swept(slot):
        for half, value in enumerate(stacked(current[1, slot])):
            high, low = split(value)
            weight[half * FPD : (half + 1) * FPD, 0:COLS] = high
            weight[half * FPD : (half + 1) * FPD, COLS : 2 * COLS] = low
        term = dot(green_hi[slot], weight[...])
        rest = dot(green_lo[slot], weight[:, 0:COLS])
        total[1] += term[:, 0:COLS] + (term[:, COLS:] + rest)

    def chunks(body):
        def one(i, _):
            body(i)
            return 0

        lax.fori_loop(0, CYC, one, 0)

    def partial_of(sweep, c, e, device):
        index = (0, 1, None, 2, 3, 4)[(2 - c) * 2 + e]
        return (
            total.at[sweep, pl.ds((c * 2 + e) * FPD, FPD)],
            part_in.at[sweep, index],
            part_send.at[sweep * 5 + index],
            part_recv.at[sweep * 5 + index],
            device,
        )

    def exchange(sweep):
        for owner in owners:
            put(partial_of, sweep, *owner)
        result = start + total[sweep, 2 * FPD : 3 * FPD, :]
        for owner in owners:
            copy(*partial_of(sweep, *owner)).wait_recv()
        for index in range(5):
            result = result + part_in[sweep, index]
        return result

    for slot in (0, 1, 3, 4, 5):
        spread(slot)

    def start_step(slot, _):
        @pl.when(slot == 1)
        def _():
            told(0, -1, 1)

        @pl.when(slot == 2)
        def _():
            arrive(0, 2, 3)
            pass_on(0, 11, 12)

        @pl.when(slot == 3)
        def _():
            arrive(0, 0, 1)
            tell(3, -3, 4)
            told(0, -2, 2)
            pass_on(0, 5, 6, 9, 10, 7, 8)

        @pl.when(slot == 5)
        def _():
            told(1, 0)

        @pl.when(slot == 6)
        def _():
            told(1, -1, 1)
            arrive(0, 4)

        @pl.when(slot == 7)
        def _():
            arrive(0, 11, 12)

        @pl.when(slot == 8)
        def _():
            told(1, -2, 2)
            arrive(0, 9, 10)
            pass_on(0, 13, 14)

        @pl.when(slot == 9)
        def _():
            told(0, -3, 3, 4)

        @pl.when(slot == 10)
        def _():
            arrive(0, 7, 8)
            pass_on(0, 15)

        @pl.when(slot == 11)
        def _():
            arrive(0, 5, 6)

        @pl.when(slot == 13)
        def _():
            told(1, -3, 3)

        @pl.when(slot == 14)
        def _():
            arrive(0, 13, 14)

        @pl.when(slot == 15)
        def _():
            told(1, 4)

        prior = slot - 1
        weigh_start(prior)
        visible(slot)

        def both(i):
            add_start(prior, i)
            make_green(slot, i)

        chunks(both)
        return 0

    visible(0)
    chunks(functools.partial(make_green, 0))
    lax.fori_loop(1, 2 * nz, start_step, 0)
    arrive(0, 15)
    weigh_start(slot_of(1, 4))
    chunks(functools.partial(add_start, slot_of(1, 4)))

    def swept_step(n, _):
        @pl.when(n == 1)
        def _():
            for part in range(2):
                arrive(1, *half(part, 0, 1))
                pass_on(1, *half(part, 5, 6, 9, 10), *half(0, 7 + part), *half(1, 7 + part))
                arrive(1, *half(part, 2, 3))
                pass_on(1, *half(part, 11, 12))

        @pl.when(n == 5)
        def _():
            arrive(1, *half(0, 4), *half(1, 4))

        @pl.when(n == 6)
        def _():
            for part in range(2):
                arrive(1, *half(part, 9, 10))
                pass_on(1, *half(part, 13, 14))
            arrive(1, *half(0, 7, 8), *half(1, 7, 8))
            pass_on(1, *half(0, 15), *half(1, 15))
            arrive(1, *half(0, 11, 12), *half(1, 11, 12))

        @pl.when(n == 10)
        def _():
            arrive(1, *half(0, 5, 6), *half(1, 5, 6))

        @pl.when(n == 13)
        def _():
            arrive(1, *half(0, 13, 14), *half(1, 13, 14))

        @pl.when(n == 15)
        def _():
            arrive(1, *half(0, 15), *half(1, 15))

        add_swept(n)
        return 0

    current[1, 0] = exchange(0)
    for part in range(2):
        pass_on(1, *half(part, 0, 1, 2, 3, 4))
    lax.fori_loop(0, 2 * nz, swept_step, 0)
    final = exchange(1)
    out_ref[...] = sum(dot(placed16, piece) for piece in split3(final))

    for place, which in sends:
        copy(*place(*which)).wait_send()


def per_device(incident, geometry, order, pairs, counts):
    nb = lax.axis_size("blk")
    nz = lax.axis_size("lane") // 4
    vmem = pl.BlockSpec(memory_space=pltpu.VMEM)
    out = pl.pallas_call(
        functools.partial(kernel, nb, nz),
        out_shape=jax.ShapeDtypeStruct((FPD, COLS), F32),
        in_specs=[vmem] * 5,
        out_specs=vmem,
        scratch_shapes=[
            pltpu.VMEM((2 * CYC, 8, LIST), F32),
            pltpu.VMEM((6, ROWS, FPD), F32),
            pltpu.VMEM((2, 2 * nz, FPD, COLS), F32),
            pltpu.VMEM((2 * nz, INFO, COLS), F32),
            pltpu.VMEM((INFO, COLS), F32),
            pltpu.VMEM((2 * FPD, 2 * COLS), BF16),
            pltpu.VMEM((2 * nz, ROWS, 2 * FPD), BF16),
            pltpu.VMEM((2 * nz, ROWS, 2 * FPD), BF16),
            pltpu.VMEM((2, ROWS, COLS), F32),
            pltpu.VMEM((2, 5, FPD, COLS), F32),
            pltpu.SemaphoreType.DMA((6,)),
            pltpu.SemaphoreType.DMA((6,)),
            pltpu.SemaphoreType.DMA((2 * nz,)),
            pltpu.SemaphoreType.DMA((2 * nz,)),
            pltpu.SemaphoreType.DMA((48,)),
            pltpu.SemaphoreType.DMA((48,)),
            pltpu.SemaphoreType.DMA((10,)),
            pltpu.SemaphoreType.DMA((10,)),
        ],
        compiler_params=pltpu.CompilerParams(
            collective_id=0, has_side_effects=True, vmem_limit_bytes=40 * 2**20
        ),
        name="sweeps",
    )(incident[0], geometry[0], order[0], pairs[0, 0], counts)
    return out[None]


def solution(mesh):
    placed = (
        P("blk", "lane", None),
        P("blk", None, "lane"),
        P("blk", "lane", None),
        P("blk", "lane", None, None),
        P("blk", "lane"),
    )
    return jax.shard_map(
        per_device, mesh=mesh, in_specs=placed, out_specs=P("blk", "lane", None), check_vma=False
    )
```

```python
import functools

import jax
import jax.numpy as jnp
from jax import lax
from jax.experimental import pallas as pl
from jax.experimental.pallas import tpu as pltpu
from jax.sharding import PartitionSpec as P

BS = 64
FB = 2
FPD = BS * FB
COLS = 128
INFO = 16
LIST = 256
PMAX = 192
CYC = 3
ROWS = CYC * 2 * FPD

F32 = jnp.float32
BF16 = jnp.bfloat16
MESH = pl.DeviceIdType.MESH
ROUND = 12582912.0
SIN = (4.442867903016683, -7.307443420820961, 3.5947880748152716, -0.7843740225385425)
COS = (
    -1.4142134965649493,
    6.978850988230643,
    -5.7394611705151934,
    1.8835629862356886,
    -0.3106981896782719,
)


def split(value):
    high = value.astype(BF16)
    return high, (value - high.astype(F32)).astype(BF16)


def split3(value):
    high, low = split(value)
    rest = value - high.astype(F32) - low.astype(F32)
    return high, low, rest.astype(BF16)


def dot(a, b):
    return jnp.dot(a, b, preferred_element_type=F32)


def kernel(
    nb,
    nz,
    inc_ref,
    geo_ref,
    order_ref,
    pairs_ref,
    count_ref,
    out_ref,
    geo_in,
    target,
    current,
    info,
    mask,
    weight,
    green_hi,
    green_lo,
    total,
    part_in,
    geo_send,
    geo_recv,
    info_send,
    info_recv,
    ring_send,
    ring_recv,
    part_send,
    part_recv,
):
    blk = lax.axis_index("blk")
    lane = lax.axis_index("lane")
    core = lane % 2
    chip = lane // 2
    z = chip % nz
    x_hi = chip // nz
    sibling = lane + 1 - 2 * core
    across = (blk, (1 - x_hi) * (2 * nz) + z * 2 + core)

    steps = {
        step: (blk, x_hi * (2 * nz) + ((z + step + nz) % nz) * 2 + core)
        for step in (1, -1, 2, -2, 3, -3, 4)
    }

    def along(step):
        return steps[step]

    def cycle(c):
        return (blk + (c - 1) + nb) % nb

    owners = [
        (c, e, (cycle(c), lane if e == 0 else sibling))
        for c, e in ((0, 0), (2, 0), (0, 1), (2, 1), (1, 1))
    ]
    near = [across, along(1), along(-1), along(2), along(-2)]

    barrier = pltpu.get_barrier_semaphore()
    for device in [d for _, _, d in owners] + near:
        pl.semaphore_signal(barrier, inc=1, device_id=device, device_id_type=MESH)

    facet = lax.broadcasted_iota(jnp.int32, (FPD, FPD), 0)
    placed = jnp.where(order_ref[...] == facet, 1.0, 0.0).astype(F32)
    placed16 = placed.astype(BF16)
    picked16 = jnp.transpose(placed).astype(BF16)
    start = dot(picked16, inc_ref[...])
    current[0, 0] = start
    info[0] = jnp.zeros((INFO, COLS), F32)
    geo_in[2] = jnp.full((8, LIST), -1.0, F32)
    pieces = split3(geo_ref[...])
    geo_in[2, 0:6, 0:FPD] = sum(dot(piece, placed16) for piece in pieces)
    live = lax.broadcasted_iota(jnp.int32, (2, PMAX), 1) < count_ref[...]
    geo_in[2, 6:8, 0:PMAX] = jnp.where(live, pairs_ref[...], -1).astype(F32)

    pl.semaphore_wait(barrier, len(owners) + len(near))

    sends = []

    def copy(source, dest, send, recv, device):
        return pltpu.make_async_remote_copy(
            src_ref=source,
            dst_ref=dest,
            send_sem=send,
            recv_sem=recv,
            device_id=device,
            device_id_type=MESH,
        )

    def put(place, *which):
        copy(*place(*which)).start()
        sends.append((place, which))

    slots = [(0, 0), (0, -1), (0, 1), (0, -2), (0, 2), (1, 0), (1, -1), (1, 1)]
    slots += [(1, -2), (1, 2), (0, -3), (0, 3), (0, 4), (1, -3), (1, 3), (1, 4)]

    def slot_of(h, d):
        return slots.index((h, 4 if d == -4 else d))

    full, top, bottom = (0, FPD), (0, FPD // 2), (FPD // 2, FPD // 2)
    hops = [
        ((0, 0), (0, -2), full, along(2)),
        ((0, 0), (0, 2), full, along(-2)),
        ((0, 0), (0, -1), full, along(1)),
        ((0, 0), (0, 1), full, along(-1)),
        ((0, 0), (1, 0), full, across),
        ((0, -2), (0, -3), full, along(1)),
        ((0, 2), (0, 3), full, along(-1)),
        ((0, -2), (0, 4), top, along(2)),
        ((0, 2), (0, 4), bottom, along(-2)),
        ((0, -2), (1, -2), full, across),
        ((0, 2), (1, 2), full, across),
        ((1, 0), (1, -1), full, along(1)),
        ((1, 0), (1, 1), full, along(-1)),
        ((1, -2), (1, -3), full, along(1)),
        ((1, 2), (1, 3), full, along(-1)),
        ((0, 4), (1, 4), full, across),
    ]

    halves = []
    for source, dest, (base, height), device in hops:
        for part in range(2):
            rows = (base + part * height // 2, height // 2)
            halves.append((source, dest, rows, device))

    def half(part, *which):
        return [2 * k + part for k in which]

    def hop(sweep, k):
        source, dest, rows, device = (hops, halves)[sweep][k]
        sem = sweep * len(hops) + k
        return (
            current.at[sweep, slot_of(*source), pl.ds(*rows)],
            current.at[sweep, slot_of(*dest), pl.ds(*rows)],
            ring_send.at[sem],
            ring_recv.at[sem],
            device,
        )

    def pass_on(sweep, *which):
        for k in which:
            put(hop, sweep, k)

    def arrive(sweep, *which):
        for k in which:
            copy(*hop(sweep, k)).wait_recv()

    def note(source, dest, device):
        there = slot_of(*dest)
        return (
            info.at[slot_of(*source)],
            info.at[there],
            info_send.at[there],
            info_recv.at[there],
            device,
        )

    def tell(*steps):
        for step in steps:
            put(note, (0, 0), (0, -step), along(step))

    def told(h, *distances):
        for d in distances:
            if h == 0:
                copy(*note((0, 0), (0, d), across)).wait_recv()
                put(note, (0, d), (1, d), across)
            else:
                copy(*note((0, d), (1, d), across)).wait_recv()

    def place_of(slot, device):
        return geo_in.at[2], geo_in.at[slot], geo_send.at[slot], geo_recv.at[slot], device

    for c, e, device in owners:
        put(place_of, (2 - c) * 2 + e, device)
    pass_on(0, 4, 2, 3, 0, 1)

    def spread(slot):
        turned = jnp.transpose(geo_in[slot, :, 0:FPD])
        for row in range(6):
            target[row, slot * FPD : (slot + 1) * FPD, :] = jnp.broadcast_to(
                turned[:, row : row + 1], (FPD, FPD)
            )

    total[...] = jnp.zeros(total.shape, F32)
    spread(2)
    for c, e, device in owners:
        copy(*place_of(c * 2 + e, device)).wait_recv()
    for c in range(CYC):
        for row in range(2):
            base = row * 6 + c * 2
            info[0, base : base + 1, :] = geo_in[c * 2, 6 + row : 7 + row, 0:128]
            info[0, base + 1 : base + 2, :] = geo_in[c * 2, 6 + row : 7 + row, 128:256]
    info[0, 12:15, :] = geo_in[2, 0:3, 0:FPD]
    tell(1, -1, 2, -2)
    put(note, (0, 0), (1, 0), across)

    lane_half = lax.broadcasted_iota(jnp.int32, (INFO, COLS), 1) // BS
    wanted_row = lax.broadcasted_iota(jnp.int32, (INFO, COLS), 0)
    wanted_part = wanted_row % 4
    wanted = (2 * (2 * chip + (core + wanted_part // 2) % 2) + wanted_part % 2).astype(F32)
    wanted = [jnp.where(wanted_row // 4 == c, wanted, -5.0) for c in range(CYC)]
    sign = jnp.where(lax.broadcasted_iota(jnp.int32, (FPD, COLS), 1) < BS, -1.0, 1.0)

    def stacked(value):
        swapped = jnp.concatenate([value[:, BS:], value[:, :BS]], axis=1)
        return value, swapped * sign

    def visible(slot):
        seen = [jnp.zeros((INFO, COLS), F32), jnp.zeros((INFO, COLS), F32)]
        told_rows = info[slot]
        for row in range(2 * CYC):
            c = row // 2
            hit = told_rows[6 + row : 7 + row, :] == wanted[c]
            for side in range(2):
                same = told_rows[row : row + 1, :] == float(2 * (2 - c) + side)
                seen[side] += jnp.where(hit & same, 1.0, 0.0)
        sums = [jnp.sum(s, axis=1, keepdims=True) for s in seen]
        mask[...] = jnp.where(lane_half == 0, sums[0], sums[1])

    def make_green(slot, i):
        place = info[slot, 12:15, :]
        for part in range(2 * FB):
            rows = pl.ds(pl.multiple_of((i * 2 * FB + part) * BS, BS), BS)
            offset = [place[k : k + 1, :] - target[k, rows, :] for k in range(3)]
            square = offset[0] * offset[0] + offset[1] * offset[1]
            square = square + offset[2] * offset[2] + 1.0
            inverse = lax.rsqrt(square)
            radius = square * inverse
            facing = sum(target[3 + k, rows, :] * offset[k] for k in range(3))
            facing = facing * mask[pl.ds(2 * FB * i + part, 1), :] * (inverse * inverse)
            turn = radius - ((radius + ROUND) - ROUND)
            power = turn * turn
            sine = turn * (((SIN[3] * power + SIN[2]) * power + SIN[1]) * power + SIN[0])
            cosine = COS[4] * power + COS[3]
            cosine = ((cosine * power + COS[2]) * power + COS[1]) * power + COS[0]
            pieces = split(facing * (1.0 - sine * sine)), split(facing * (sine * cosine))
            for half in range(2):
                lanes = pl.ds(half * FPD, FPD)
                green_hi[slot, rows, lanes], green_lo[slot, rows, lanes] = pieces[half]

    def weigh_start(slot):
        for half, value in enumerate(stacked(current[0, slot])):
            weight[half * FPD : (half + 1) * FPD, 0:COLS] = value.astype(BF16)

    def add_start(slot, i):
        rows = pl.ds(pl.multiple_of(i * 2 * FPD, 2 * FPD), 2 * FPD)
        both = jnp.concatenate([green_hi[slot, rows, :], green_lo[slot, rows, :]], axis=0)
        term = dot(both, weight[:, 0:COLS])
        total[0, rows, :] += term[0 : 2 * FPD] + term[2 * FPD :]

    def add_swept(slot):
        for half, value in enumerate(stacked(current[1, slot])):
            high, low = split(value)
            weight[half * FPD : (half + 1) * FPD, 0:COLS] = high
            weight[half * FPD : (half + 1) * FPD, COLS : 2 * COLS] = low
        term = dot(green_hi[slot], weight[...])
        rest = dot(green_lo[slot], weight[:, 0:COLS])
        total[1] += term[:, 0:COLS] + (term[:, COLS:] + rest)

    def chunks(body):
        def one(i, _):
            body(i)
            return 0

        lax.fori_loop(0, CYC, one, 0)

    def partial_of(sweep, part, c, e, device):
        index = (0, 1, None, 2, 3, 4)[(2 - c) * 2 + e]
        sem = (sweep * 2 + part) * 5 + index
        return (
            total.at[sweep, pl.ds((c * 2 + e) * FPD + part * BS, BS)],
            part_in.at[sweep, index, pl.ds(part * BS, BS)],
            part_send.at[sem],
            part_recv.at[sem],
            device,
        )

    def exchange(sweep, take):
        for part in range(2):
            for owner in owners:
                put(partial_of, sweep, part, *owner)
        for part in range(2):
            rows = slice(part * BS, (part + 1) * BS)
            result = current[0, 0, rows, :]
            result = result + total[sweep, 2 * FPD + part * BS : 2 * FPD + (part + 1) * BS, :]
            for owner in owners:
                copy(*partial_of(sweep, part, *owner)).wait_recv()
            for index in range(5):
                result = result + part_in[sweep, index, rows, :]
            take(part, rows, result)

    def sweep_on(part, rows, result):
        current[1, 0, rows, :] = result
        pass_on(1, *half(part, 4, 2, 3, 0, 1))

    finals = []

    def finish(part, rows, result):
        finals.append(result)


    for slot in (0, 1, 3, 4, 5):
        spread(slot)

    def start_step(slot, _):
        @pl.when(slot == 1)
        def _():
            told(0, -1, 1)

        @pl.when(slot == 2)
        def _():
            arrive(0, 4)
            pass_on(0, 11, 12)
            arrive(0, 2, 3)

        @pl.when(slot == 3)
        def _():
            arrive(0, 0, 1)
            tell(3, -3, 4)
            told(0, -2, 2)
            pass_on(0, 5, 6, 9, 10, 7, 8)

        @pl.when(slot == 5)
        def _():
            told(1, 0)

        @pl.when(slot == 6)
        def _():
            told(1, -1, 1)

        @pl.when(slot == 7)
        def _():
            arrive(0, 11, 12)

        @pl.when(slot == 8)
        def _():
            told(1, -2, 2)
            arrive(0, 9, 10)
            pass_on(0, 13, 14)

        @pl.when(slot == 9)
        def _():
            told(0, -3, 3, 4)

        @pl.when(slot == 10)
        def _():
            arrive(0, 7, 8)
            pass_on(0, 15)

        @pl.when(slot == 11)
        def _():
            arrive(0, 5, 6)

        @pl.when(slot == 13)
        def _():
            told(1, -3, 3)

        @pl.when(slot == 14)
        def _():
            arrive(0, 13, 14)

        @pl.when(slot == 15)
        def _():
            told(1, 4)

        prior = slot - 1
        weigh_start(prior)
        visible(slot)

        def both(i):
            add_start(prior, i)
            make_green(slot, i)

        chunks(both)
        return 0

    visible(0)
    chunks(functools.partial(make_green, 0))
    lax.fori_loop(1, 2 * nz, start_step, 0)
    arrive(0, 15)
    weigh_start(slot_of(1, 4))
    chunks(functools.partial(add_start, slot_of(1, 4)))

    def swept_step(n, _):
        @pl.when(n == 1)
        def _():
            for part in range(2):
                arrive(1, *half(part, 4))
                pass_on(1, *half(part, 11, 12))
                arrive(1, *half(part, 2, 3))
                arrive(1, *half(part, 0, 1))
                pass_on(1, *half(part, 5, 6, 9, 10), *half(0, 7 + part), *half(1, 7 + part))

        @pl.when(n == 6)
        def _():
            for part in range(2):
                arrive(1, *half(part, 9, 10))
                pass_on(1, *half(part, 13, 14))
            arrive(1, *half(0, 7, 8), *half(1, 7, 8))
            pass_on(1, *half(0, 15), *half(1, 15))
            arrive(1, *half(0, 11, 12), *half(1, 11, 12))

        @pl.when(n == 10)
        def _():
            arrive(1, *half(0, 5, 6), *half(1, 5, 6))

        @pl.when(n == 13)
        def _():
            arrive(1, *half(0, 13, 14), *half(1, 13, 14))

        @pl.when(n == 15)
        def _():
            arrive(1, *half(0, 15), *half(1, 15))

        add_swept(n)
        return 0

    exchange(0, sweep_on)
    lax.fori_loop(0, 2 * nz, swept_step, 0)
    exchange(1, finish)
    final = jnp.concatenate(finals, axis=0)
    out_ref[...] = sum(dot(placed16, piece) for piece in split3(final))

    for place, which in sends:
        copy(*place(*which)).wait_send()


def per_device(incident, geometry, order, pairs, counts):
    nb = lax.axis_size("blk")
    nz = lax.axis_size("lane") // 4
    vmem = pl.BlockSpec(memory_space=pltpu.VMEM)
    out = pl.pallas_call(
        functools.partial(kernel, nb, nz),
        out_shape=jax.ShapeDtypeStruct((FPD, COLS), F32),
        in_specs=[vmem] * 5,
        out_specs=vmem,
        scratch_shapes=[
            pltpu.VMEM((2 * CYC, 8, LIST), F32),
            pltpu.VMEM((6, ROWS, FPD), F32),
            pltpu.VMEM((2, 2 * nz, FPD, COLS), F32),
            pltpu.VMEM((2 * nz, INFO, COLS), F32),
            pltpu.VMEM((INFO, COLS), F32),
            pltpu.VMEM((2 * FPD, 2 * COLS), BF16),
            pltpu.VMEM((2 * nz, ROWS, 2 * FPD), BF16),
            pltpu.VMEM((2 * nz, ROWS, 2 * FPD), BF16),
            pltpu.VMEM((2, ROWS, COLS), F32),
            pltpu.VMEM((2, 5, FPD, COLS), F32),
            pltpu.SemaphoreType.DMA((6,)),
            pltpu.SemaphoreType.DMA((6,)),
            pltpu.SemaphoreType.DMA((2 * nz,)),
            pltpu.SemaphoreType.DMA((2 * nz,)),
            pltpu.SemaphoreType.DMA((48,)),
            pltpu.SemaphoreType.DMA((48,)),
            pltpu.SemaphoreType.DMA((20,)),
            pltpu.SemaphoreType.DMA((20,)),
        ],
        compiler_params=pltpu.CompilerParams(
            collective_id=0, has_side_effects=True, vmem_limit_bytes=40 * 2**20
        ),
        name="sweeps",
    )(incident[0], geometry[0], order[0], pairs[0, 0], counts)
    return out[None]


def solution(mesh):
    placed = (
        P("blk", "lane", None),
        P("blk", None, "lane"),
        P("blk", "lane", None),
        P("blk", "lane", None, None),
        P("blk", "lane"),
    )
    return jax.shard_map(
        per_device, mesh=mesh, in_specs=placed, out_specs=P("blk", "lane", None), check_vma=False
    )
```

```python
import functools

import jax
import jax.numpy as jnp
from jax import lax
from jax.experimental import pallas as pl
from jax.experimental.pallas import tpu as pltpu
from jax.sharding import PartitionSpec as P

BS = 64
FB = 2
FPD = BS * FB
COLS = 128
INFO = 16
LIST = 256
PMAX = 192
CYC = 3
ROWS = CYC * 2 * FPD

F32 = jnp.float32
BF16 = jnp.bfloat16
MESH = pl.DeviceIdType.MESH
ROUND = 12582912.0
SIN = (4.442867903016683, -7.307443420820961, 3.5947880748152716, -0.7843740225385425)
COS = (
    -1.4142134965649493,
    6.978850988230643,
    -5.7394611705151934,
    1.8835629862356886,
    -0.3106981896782719,
)


def split(value):
    high = value.astype(BF16)
    return high, (value - high.astype(F32)).astype(BF16)


def split3(value):
    high, low = split(value)
    rest = value - high.astype(F32) - low.astype(F32)
    return high, low, rest.astype(BF16)


def dot(a, b):
    return jnp.dot(a, b, preferred_element_type=F32)


def kernel(
    nb,
    nz,
    inc_ref,
    geo_ref,
    order_ref,
    pairs_ref,
    count_ref,
    out_ref,
    geo_in,
    target,
    current,
    info,
    mask,
    weight,
    green_hi,
    green_lo,
    total,
    part_in,
    geo_send,
    geo_recv,
    info_send,
    info_recv,
    ring_send,
    ring_recv,
    part_send,
    part_recv,
):
    blk = lax.axis_index("blk")
    lane = lax.axis_index("lane")
    core = lane % 2
    chip = lane // 2
    z = chip % nz
    x_hi = chip // nz
    sibling = lane + 1 - 2 * core
    across = (blk, (1 - x_hi) * (2 * nz) + z * 2 + core)

    steps = {
        step: (blk, x_hi * (2 * nz) + ((z + step + nz) % nz) * 2 + core)
        for step in (1, -1, 2, -2, 3, -3, 4)
    }

    def along(step):
        return steps[step]

    def cycle(c):
        return (blk + (c - 1) + nb) % nb

    owners = [
        (c, e, (cycle(c), lane if e == 0 else sibling))
        for c, e in ((0, 0), (2, 0), (0, 1), (2, 1), (1, 1))
    ]
    near = [across, along(1), along(-1), along(2), along(-2)]

    barrier = pltpu.get_barrier_semaphore()
    for device in [d for _, _, d in owners] + near:
        pl.semaphore_signal(barrier, inc=1, device_id=device, device_id_type=MESH)

    facet = lax.broadcasted_iota(jnp.int32, (FPD, FPD), 0)
    placed = jnp.where(order_ref[...] == facet, 1.0, 0.0).astype(F32)
    placed16 = placed.astype(BF16)
    picked16 = jnp.transpose(placed).astype(BF16)
    start = dot(picked16, inc_ref[...])
    current[0, 0] = start
    info[0] = jnp.zeros((INFO, COLS), F32)
    geo_in[2] = jnp.full((8, LIST), -1.0, F32)
    pieces = split3(geo_ref[...])
    geo_in[2, 0:6, 0:FPD] = sum(dot(piece, placed16) for piece in pieces)
    live = lax.broadcasted_iota(jnp.int32, (2, PMAX), 1) < count_ref[...]
    geo_in[2, 6:8, 0:PMAX] = jnp.where(live, pairs_ref[...], -1).astype(F32)

    pl.semaphore_wait(barrier, len(owners) + len(near))

    sends = []

    def copy(source, dest, send, recv, device):
        return pltpu.make_async_remote_copy(
            src_ref=source,
            dst_ref=dest,
            send_sem=send,
            recv_sem=recv,
            device_id=device,
            device_id_type=MESH,
        )

    def put(place, *which):
        copy(*place(*which)).start()
        sends.append((place, which))

    slots = [(0, 0), (0, -1), (0, 1), (0, -2), (0, 2), (1, 0), (1, -1), (1, 1)]
    slots += [(1, -2), (1, 2), (0, -3), (0, 3), (0, 4), (1, -3), (1, 3), (1, 4)]

    def slot_of(h, d):
        return slots.index((h, 4 if d == -4 else d))

    full, top, bottom = (0, FPD), (0, FPD // 2), (FPD // 2, FPD // 2)
    hops = [
        ((0, 0), (0, -2), full, along(2)),
        ((0, 0), (0, 2), full, along(-2)),
        ((0, 0), (0, -1), full, along(1)),
        ((0, 0), (0, 1), full, along(-1)),
        ((0, 0), (1, 0), full, across),
        ((0, -2), (0, -3), full, along(1)),
        ((0, 2), (0, 3), full, along(-1)),
        ((0, -2), (0, 4), top, along(2)),
        ((0, 2), (0, 4), bottom, along(-2)),
        ((0, -2), (1, -2), full, across),
        ((0, 2), (1, 2), full, across),
        ((1, 0), (1, -1), full, along(1)),
        ((1, 0), (1, 1), full, along(-1)),
        ((1, -2), (1, -3), full, along(1)),
        ((1, 2), (1, 3), full, along(-1)),
        ((1, -2), (1, 4), top, along(2)),
        ((1, 2), (1, 4), bottom, along(-2)),
    ]

    halves = []
    for source, dest, (base, height), device in hops:
        for part in range(2):
            rows = (base + part * height // 2, height // 2)
            halves.append((source, dest, rows, device))

    def half(part, *which):
        return [2 * k + part for k in which]

    def hop(sweep, k):
        source, dest, rows, device = (hops, halves)[sweep][k]
        sem = sweep * len(hops) + k
        return (
            current.at[sweep, slot_of(*source), pl.ds(*rows)],
            current.at[sweep, slot_of(*dest), pl.ds(*rows)],
            ring_send.at[sem],
            ring_recv.at[sem],
            device,
        )

    def pass_on(sweep, *which):
        for k in which:
            put(hop, sweep, k)

    def arrive(sweep, *which):
        for k in which:
            copy(*hop(sweep, k)).wait_recv()

    def note(source, dest, device):
        there = slot_of(*dest)
        return (
            info.at[slot_of(*source)],
            info.at[there],
            info_send.at[there],
            info_recv.at[there],
            device,
        )

    def tell(*steps):
        for step in steps:
            put(note, (0, 0), (0, -step), along(step))

    def told(h, *distances):
        for d in distances:
            if h == 0:
                copy(*note((0, 0), (0, d), across)).wait_recv()
                put(note, (0, d), (1, d), across)
            else:
                copy(*note((0, d), (1, d), across)).wait_recv()

    def place_of(slot, device):
        return geo_in.at[2], geo_in.at[slot], geo_send.at[slot], geo_recv.at[slot], device

    for c, e, device in owners:
        put(place_of, (2 - c) * 2 + e, device)
    pass_on(0, 4, 2, 3, 0, 1)

    def spread(slot):
        turned = jnp.transpose(geo_in[slot, :, 0:FPD])
        for row in range(6):
            target[row, slot * FPD : (slot + 1) * FPD, :] = jnp.broadcast_to(
                turned[:, row : row + 1], (FPD, FPD)
            )

    total[...] = jnp.zeros(total.shape, F32)
    spread(2)
    for c, e, device in owners:
        copy(*place_of(c * 2 + e, device)).wait_recv()
    for c in range(CYC):
        for row in range(2):
            base = row * 6 + c * 2
            info[0, base : base + 1, :] = geo_in[c * 2, 6 + row : 7 + row, 0:128]
            info[0, base + 1 : base + 2, :] = geo_in[c * 2, 6 + row : 7 + row, 128:256]
    info[0, 12:15, :] = geo_in[2, 0:3, 0:FPD]
    tell(1, -1, 2, -2)
    put(note, (0, 0), (1, 0), across)

    lane_half = lax.broadcasted_iota(jnp.int32, (INFO, COLS), 1) // BS
    wanted_row = lax.broadcasted_iota(jnp.int32, (INFO, COLS), 0)
    wanted_part = wanted_row % 4
    wanted = (2 * (2 * chip + (core + wanted_part // 2) % 2) + wanted_part % 2).astype(F32)
    wanted = [jnp.where(wanted_row // 4 == c, wanted, -5.0) for c in range(CYC)]
    sign = jnp.where(lax.broadcasted_iota(jnp.int32, (FPD, COLS), 1) < BS, -1.0, 1.0)

    def stacked(value):
        swapped = jnp.concatenate([value[:, BS:], value[:, :BS]], axis=1)
        return value, swapped * sign

    def visible(slot):
        seen = [jnp.zeros((INFO, COLS), F32), jnp.zeros((INFO, COLS), F32)]
        told_rows = info[slot]
        for row in range(2 * CYC):
            c = row // 2
            hit = told_rows[6 + row : 7 + row, :] == wanted[c]
            for side in range(2):
                same = told_rows[row : row + 1, :] == float(2 * (2 - c) + side)
                seen[side] += jnp.where(hit & same, 1.0, 0.0)
        sums = [jnp.sum(s, axis=1, keepdims=True) for s in seen]
        mask[...] = jnp.where(lane_half == 0, sums[0], sums[1])

    def make_green(slot, i):
        place = info[slot, 12:15, :]
        for part in range(2 * FB):
            rows = pl.ds(pl.multiple_of((i * 2 * FB + part) * BS, BS), BS)
            offset = [place[k : k + 1, :] - target[k, rows, :] for k in range(3)]
            square = offset[0] * offset[0] + offset[1] * offset[1]
            square = square + offset[2] * offset[2] + 1.0
            inverse = lax.rsqrt(square)
            radius = square * inverse
            facing = sum(target[3 + k, rows, :] * offset[k] for k in range(3))
            facing = facing * mask[pl.ds(2 * FB * i + part, 1), :] * (inverse * inverse)
            turn = radius - ((radius + ROUND) - ROUND)
            power = turn * turn
            sine = turn * (((SIN[3] * power + SIN[2]) * power + SIN[1]) * power + SIN[0])
            cosine = COS[4] * power + COS[3]
            cosine = ((cosine * power + COS[2]) * power + COS[1]) * power + COS[0]
            pieces = split(facing * (1.0 - sine * sine)), split(facing * (sine * cosine))
            for half in range(2):
                lanes = pl.ds(half * FPD, FPD)
                green_hi[slot, rows, lanes], green_lo[slot, rows, lanes] = pieces[half]

    def weigh_start(slot):
        for half, value in enumerate(stacked(current[0, slot])):
            weight[half * FPD : (half + 1) * FPD, 0:COLS] = value.astype(BF16)

    def add_start(slot, i):
        rows = pl.ds(pl.multiple_of(i * 2 * FPD, 2 * FPD), 2 * FPD)
        both = jnp.concatenate([green_hi[slot, rows, :], green_lo[slot, rows, :]], axis=0)
        term = dot(both, weight[:, 0:COLS])
        total[0, rows, :] += term[0 : 2 * FPD] + term[2 * FPD :]

    def add_swept(slot):
        for half, value in enumerate(stacked(current[1, slot])):
            high, low = split(value)
            weight[half * FPD : (half + 1) * FPD, 0:COLS] = high
            weight[half * FPD : (half + 1) * FPD, COLS : 2 * COLS] = low
        term = dot(green_hi[slot], weight[...])
        rest = dot(green_lo[slot], weight[:, 0:COLS])
        total[1] += term[:, 0:COLS] + (term[:, COLS:] + rest)

    def chunks(body):
        def one(i, _):
            body(i)
            return 0

        lax.fori_loop(0, CYC, one, 0)

    def partial_of(sweep, part, c, e, device):
        index = (0, 1, None, 2, 3, 4)[(2 - c) * 2 + e]
        sem = (sweep * 2 + part) * 5 + index
        return (
            total.at[sweep, pl.ds((c * 2 + e) * FPD + part * BS, BS)],
            part_in.at[sweep, index, pl.ds(part * BS, BS)],
            part_send.at[sem],
            part_recv.at[sem],
            device,
        )

    def exchange(sweep, take):
        for part in range(2):
            for owner in owners:
                put(partial_of, sweep, part, *owner)
        for part in range(2):
            rows = slice(part * BS, (part + 1) * BS)
            result = current[0, 0, rows, :]
            result = result + total[sweep, 2 * FPD + part * BS : 2 * FPD + (part + 1) * BS, :]
            for owner in owners:
                copy(*partial_of(sweep, part, *owner)).wait_recv()
            for index in range(5):
                result = result + part_in[sweep, index, rows, :]
            take(part, rows, result)

    def sweep_on(part, rows, result):
        current[1, 0, rows, :] = result
        pass_on(1, *half(part, 4, 2, 3, 0, 1))

    finals = []

    def finish(part, rows, result):
        finals.append(result)


    for slot in (0, 1, 3, 4, 5):
        spread(slot)

    def start_step(slot, _):
        @pl.when(slot == 1)
        def _():
            told(0, -1, 1)

        @pl.when(slot == 2)
        def _():
            arrive(0, 4)
            pass_on(0, 11, 12)
            arrive(0, 2, 3)

        @pl.when(slot == 3)
        def _():
            arrive(0, 0, 1)
            tell(3, -3, 4)
            told(0, -2, 2)
            pass_on(0, 5, 6, 9, 10, 7, 8)

        @pl.when(slot == 5)
        def _():
            told(1, 0)

        @pl.when(slot == 6)
        def _():
            told(1, -1, 1)

        @pl.when(slot == 7)
        def _():
            arrive(0, 11, 12)

        @pl.when(slot == 8)
        def _():
            told(1, -2, 2)
            arrive(0, 9, 10)
            pass_on(0, 13, 14, 15, 16)

        @pl.when(slot == 9)
        def _():
            told(0, -3, 3, 4)

        @pl.when(slot == 10)
        def _():
            arrive(0, 7, 8)

        @pl.when(slot == 11)
        def _():
            arrive(0, 5, 6)

        @pl.when(slot == 13)
        def _():
            told(1, -3, 3)

        @pl.when(slot == 14)
        def _():
            arrive(0, 13, 14)

        @pl.when(slot == 15)
        def _():
            told(1, 4)

        prior = slot - 1
        weigh_start(prior)
        visible(slot)

        def both(i):
            add_start(prior, i)
            make_green(slot, i)

        chunks(both)
        return 0

    visible(0)
    chunks(functools.partial(make_green, 0))
    lax.fori_loop(1, 2 * nz, start_step, 0)
    arrive(0, 15, 16)
    weigh_start(slot_of(1, 4))
    chunks(functools.partial(add_start, slot_of(1, 4)))

    def swept_step(n, _):
        @pl.when(n == 1)
        def _():
            for part in range(2):
                arrive(1, *half(part, 4))
                pass_on(1, *half(part, 11, 12))
                arrive(1, *half(part, 2, 3))
                arrive(1, *half(part, 0, 1))
                pass_on(1, *half(part, 5, 6, 9, 10), *half(0, 7 + part), *half(1, 7 + part))

        @pl.when(n == 6)
        def _():
            for part in range(2):
                arrive(1, *half(part, 9, 10))
                pass_on(1, *half(part, 13, 14), *half(0, 15 + part), *half(1, 15 + part))
            arrive(1, *half(0, 7, 8), *half(1, 7, 8))
            arrive(1, *half(0, 11, 12), *half(1, 11, 12))

        @pl.when(n == 10)
        def _():
            arrive(1, *half(0, 5, 6), *half(1, 5, 6))

        @pl.when(n == 13)
        def _():
            arrive(1, *half(0, 13, 14), *half(1, 13, 14))

        @pl.when(n == 15)
        def _():
            arrive(1, *half(0, 15, 16), *half(1, 15, 16))

        add_swept(n)
        return 0

    exchange(0, sweep_on)
    lax.fori_loop(0, 2 * nz, swept_step, 0)
    exchange(1, finish)
    final = jnp.concatenate(finals, axis=0)
    out_ref[...] = sum(dot(placed16, piece) for piece in split3(final))

    for place, which in sends:
        copy(*place(*which)).wait_send()


def per_device(incident, geometry, order, pairs, counts):
    nb = lax.axis_size("blk")
    nz = lax.axis_size("lane") // 4
    vmem = pl.BlockSpec(memory_space=pltpu.VMEM)
    out = pl.pallas_call(
        functools.partial(kernel, nb, nz),
        out_shape=jax.ShapeDtypeStruct((FPD, COLS), F32),
        in_specs=[vmem] * 5,
        out_specs=vmem,
        scratch_shapes=[
            pltpu.VMEM((2 * CYC, 8, LIST), F32),
            pltpu.VMEM((6, ROWS, FPD), F32),
            pltpu.VMEM((2, 2 * nz, FPD, COLS), F32),
            pltpu.VMEM((2 * nz, INFO, COLS), F32),
            pltpu.VMEM((INFO, COLS), F32),
            pltpu.VMEM((2 * FPD, 2 * COLS), BF16),
            pltpu.VMEM((2 * nz, ROWS, 2 * FPD), BF16),
            pltpu.VMEM((2 * nz, ROWS, 2 * FPD), BF16),
            pltpu.VMEM((2, ROWS, COLS), F32),
            pltpu.VMEM((2, 5, FPD, COLS), F32),
            pltpu.SemaphoreType.DMA((6,)),
            pltpu.SemaphoreType.DMA((6,)),
            pltpu.SemaphoreType.DMA((2 * nz,)),
            pltpu.SemaphoreType.DMA((2 * nz,)),
            pltpu.SemaphoreType.DMA((51,)),
            pltpu.SemaphoreType.DMA((51,)),
            pltpu.SemaphoreType.DMA((20,)),
            pltpu.SemaphoreType.DMA((20,)),
        ],
        compiler_params=pltpu.CompilerParams(
            collective_id=0, has_side_effects=True, vmem_limit_bytes=40 * 2**20
        ),
        name="sweeps",
    )(incident[0], geometry[0], order[0], pairs[0, 0], counts)
    return out[None]


def solution(mesh):
    placed = (
        P("blk", "lane", None),
        P("blk", None, "lane"),
        P("blk", "lane", None),
        P("blk", "lane", None, None),
        P("blk", "lane"),
    )
    return jax.shard_map(
        per_device, mesh=mesh, in_specs=placed, out_specs=P("blk", "lane", None), check_vma=False
    )
```
